32 devices in a mesh: groups: 2 (over x), node: 16 (over z, y, core).
Axes of the slice: x: 2, y: 2, z: 4, core: 2. Of those that a mesh axis runs over, the one named last changes fastest.
Arguments:
- tokens: bfloat16 [4096, 2048], P(('groups', 'node')), parts along dimension 0, may hold values from -6 to 6
- routes: int32 [4096, 2], P(('groups', 'node')), parts along dimension 0, may hold values from 0 to 7, as said below
- gate_values: float32 [4096, 2], P(('groups', 'node')), parts along dimension 0, may hold values from 0.1 to 1
- cotangent: bfloat16 [4096, 2048], P(('groups', 'node')), parts along dimension 0, may hold values from -6 to 6
- gate_up: bfloat16 [16, 2, 704, 2048], P('node'), may hold values from -0.125 to 0.125
- down_weight: bfloat16 [16, 704, 2048], P('node'), may hold values from -0.15625 to 0.15625
Outputs:
- layer_out: bfloat16 [4096, 2048], P(('groups', 'node')), parts along dimension 0
- token_grad: bfloat16 [4096, 2048], P(('groups', 'node')), parts along dimension 0
- gate_grad: float32 [4096, 2], P(('groups', 'node')), parts along dimension 0
The draws below stay inside these ranges and needn't reach their ends.
There are 2 independent parts, one for each index of `groups`. The reference program is written for one: setup_inputs(seed, part) draws one part's arguments, and reference() takes and returns one part's arrays. A program takes and returns all parts, laid end to end along the dimension named above; an argument that names none is the same for every part. Nothing has to cross between parts.
Inputs may be any that keep to these rules, and one draw needn't show every extreme that they name: `routes`: each token names 2 different experts. Among the tokens of one index of node, half of the experts are named by exactly 48 tokens each and the other half by exactly 16 each; one expert is among the first half on every index of node.
All inputs are finite; a program needn't handle non-finite values.
Results may differ from the reference program's by a relative error of at most 0.0072.
Values may be sent and summed in bfloat16 or wider, within the bound.
A program may use at most 128 MiB of HBM per device.

```python
import jax
import jax.numpy as jnp
from jax import lax

D = 2048
FF = 1408
TOP = 2
TOK_DEV = 128
EXPERTS = 8
FF_HALF = 704
CAP = 48
EXP_ROWS = 768
TOKENS = 2048
N_NODE = 16


def draw_routes(key, part):
    key = jax.random.fold_in(key, 11)
    block_count = TOKENS // TOK_DEV
    average = TOK_DEV * TOP // EXPERTS
    high_load = 3 * average // 2
    low_load = average // 2
    hot_expert = jax.random.randint(jax.random.fold_in(key, 1), (), 0, EXPERTS)
    split_at = EXPERTS // 2 * high_load

    def one_block(sub):
        first_key, second_key = jax.random.split(sub)
        shuffled = jax.random.permutation(first_key, EXPERTS)
        priority = jnp.where(shuffled == hot_expert, -1, jnp.arange(EXPERTS))
        ordered = shuffled[jnp.argsort(priority, stable=True)]
        positions = jnp.arange(TOK_DEV * TOP)
        ranking = jnp.where(positions < split_at, positions // high_load, EXPERTS // 2 + (positions - split_at) // low_load)
        chosen = ordered[ranking]
        grid = chosen.reshape(TOP, TOK_DEV).T
        token_order = jax.random.permutation(second_key, TOK_DEV)
        return grid[token_order]
    block_keys = jax.random.split(jax.random.fold_in(key, 2), block_count)
    return jax.vmap(one_block)(block_keys).reshape(TOKENS, TOP).astype(jnp.int32)


def block_levels(own_key, shape, cuts, smallest, largest):
    level = 1.0
    for dim, parts in cuts:
        heights = jax.random.uniform(jax.random.fold_in(jax.random.fold_in(own_key, 6), dim), (parts,), jnp.float32, smallest / len(cuts), largest / len(cuts))
        level = level * jnp.repeat(jnp.exp(heights), shape[dim] // parts).reshape((-1,) + (1,) * (len(shape) - 1 - dim))
    return level


def gaussian(stream_key, shape, spread, limit, cuts=(), held_as=jnp.bfloat16):
    loudness = block_levels(stream_key, shape, cuts, -0.22, 0.18) if cuts else 1.0
    values = jax.random.normal(stream_key, shape, jnp.float32) * spread * loudness
    return jnp.minimum(jnp.maximum(values, -limit), limit).astype(held_as)


def setup_inputs(seed: int = 0, part: int = 0) -> dict:
    key_of = jax.random.split(jax.random.key(seed), 7)
    own_keys = jax.random.split(jax.random.fold_in(key_of[6], part), 7)
    tokens = gaussian(own_keys[0], (TOKENS, D), 1.0, 6.0, ((0, 16),))
    routes = draw_routes(jax.random.fold_in(jax.random.fold_in(key_of[6], part), 71), part)
    gate_values = jnp.clip(0.1 + 0.9 * jax.random.uniform(own_keys[2], (TOKENS, TOP), jnp.float32) ** block_levels(own_keys[2], (TOKENS, TOP), ((0, 16),), -0.2, 0.2), 0.1, 1.0)
    cotangent = gaussian(own_keys[3], (TOKENS, D), 1.0, 6.0, ((0, 16),))
    gate_up = gaussian(key_of[4], (2 * EXPERTS, 2, FF_HALF, D), D ** -0.5, 0.125, ((0, 16),))
    down_weight = gaussian(key_of[5], (2 * EXPERTS, FF_HALF, D), FF ** -0.5, 0.15625, ((0, 16),))
    return {"tokens": tokens, "routes": routes, "gate_values": gate_values, "cotangent": cotangent, "gate_up": gate_up, "down_weight": down_weight}


def half_pass(inputs, scaled, weights, down_rows):
    half_units = down_rows.shape[0]
    projected = jnp.dot(inputs, weights.T, preferred_element_type=jnp.float32)
    gate_part = projected[:, :half_units]
    up_part = projected[:, half_units:]
    sigmoid_gate = jax.nn.sigmoid(gate_part)
    activated = gate_part * sigmoid_gate
    hidden = (activated * up_part).astype(jnp.bfloat16)
    partial_out = jnp.dot(hidden, down_rows, preferred_element_type=jnp.float32).astype(jnp.bfloat16)
    d_hidden = jnp.dot(scaled, down_rows.T, preferred_element_type=jnp.float32)
    d_gate = d_hidden * up_part * sigmoid_gate * (1.0 + gate_part * (1.0 - sigmoid_gate))
    d_up = d_hidden * activated
    d_both = jnp.concatenate([d_gate, d_up], axis=1).astype(jnp.bfloat16)
    d_partial = jnp.dot(d_both, weights, preferred_element_type=jnp.float32).astype(jnp.bfloat16)
    return partial_out, d_partial


def reference(tokens, routes, gate_values, cotangent, gate_up, down_weight):
    pair_count = TOKENS * TOP
    flat_routes = routes.reshape(N_NODE, TOK_DEV * TOP)
    onehot = (flat_routes[:, :, None] == jnp.arange(EXPERTS, dtype=jnp.int32)[None, None, :]).astype(jnp.int32)
    before = jnp.cumsum(onehot, axis=1) - onehot
    slot_index = jnp.sum(before * onehot, axis=2).reshape(pair_count).astype(jnp.int32)
    expert = routes.reshape(pair_count).astype(jnp.int32)
    number = jnp.arange(pair_count, dtype=jnp.int32)
    row_place = (number // (TOK_DEV * TOP)) * CAP + slot_index
    row_table = jnp.full((EXPERTS, EXP_ROWS), pair_count, jnp.int32).at[expert, row_place].set(number)
    padded_tokens = jnp.concatenate([tokens, jnp.zeros((1, D), jnp.bfloat16)], axis=0)
    padded_cot = jnp.concatenate([cotangent, jnp.zeros((1, D), jnp.bfloat16)], axis=0)
    padded_gates = jnp.concatenate([gate_values.reshape(pair_count), jnp.zeros((1,), jnp.float32)], axis=0)
    half_units = FF // 2

    def per_expert(packed):
        expert_id, buffer_rows = packed
        is_live = buffer_rows < pair_count
        token_ids = jnp.where(is_live, buffer_rows // TOP, TOKENS).astype(jnp.int32)
        inputs = padded_tokens[token_ids]
        scaled = (padded_gates[buffer_rows][:, None] * padded_cot[token_ids].astype(jnp.float32)).astype(jnp.bfloat16)
        out_sum = jnp.zeros((EXP_ROWS, D), jnp.float32)
        grad_sum = jnp.zeros((EXP_ROWS, D), jnp.float32)
        for half in range(2):
            index = (2 * expert_id + half).astype(jnp.int32)
            weights = lax.dynamic_index_in_dim(gate_up, index, 0, keepdims=False).reshape(2 * half_units, D)
            down_rows = lax.dynamic_index_in_dim(down_weight, index, 0, keepdims=False)
            partial_out, d_partial = half_pass(inputs, scaled, weights, down_rows)
            out_sum = out_sum + partial_out.astype(jnp.float32)
            grad_sum = grad_sum + d_partial.astype(jnp.float32)
        return out_sum.astype(jnp.bfloat16), grad_sum.astype(jnp.bfloat16)

    expert_out, d_expert = lax.map(per_expert, (jnp.arange(EXPERTS, dtype=jnp.int32), row_table))
    out_pairs = expert_out[expert, row_place].astype(jnp.float32).reshape(TOKENS, TOP, D)
    layer_out = jnp.sum(gate_values[:, :, None] * out_pairs, axis=1).astype(jnp.bfloat16)
    gate_grad = jnp.sum(out_pairs * cotangent.astype(jnp.float32)[:, None, :], axis=2)
    grad_pairs = d_expert[expert, row_place].astype(jnp.float32).reshape(TOKENS, TOP, D)
    token_grad = jnp.sum(grad_pairs, axis=1).astype(jnp.bfloat16)
    return layer_out, token_grad, gate_grad
```

```python
import functools

import jax
import jax.numpy as jnp
from jax import lax
from jax.experimental import pallas as pl
from jax.experimental.pallas import tpu as pltpu
from jax.sharding import PartitionSpec as P

MESH = pl.DeviceIdType.MESH
SEND_ORDER = (4, 5, 1, 6, 7, 2, 3)
BATCHES = (0, 4, 6, 2)
TILE = 256


def flip(index, step):
    bit = 1
    while bit <= step:
        if step & bit:
            index = index + (1 - 2 * ((index // bit) % 2)) * bit
        bit *= 2
    return index


def kernel(
    chips, capacity, tok_ref, cot_ref, routes_ref, routes_t_ref, gates_ref, gates_t_ref, gu_ref, dw_ref,
    out_ref, tgrad_ref, ggrad_ref,
    weights, packed, arrived, results, returned, acc_out, acc_grad,
    w_local, w_send, w_recv, in_send, in_recv, back_send, back_recv, self_sem,
):
    tok_rows, features = tok_ref.shape
    half = dw_ref.shape[1]
    units = 2 * half
    node = lax.axis_index("node")
    chip = node // 2
    core = node % 2
    sibling = chip * 2 + 1 - core

    def device(step):
        return {"node": flip(chip, step) * 2 + core}

    barrier = pltpu.get_barrier_semaphore()
    for step in range(1, chips):
        pl.semaphore_signal(barrier, inc=1, device_id=device(step), device_id_type=MESH)
    pl.semaphore_signal(barrier, inc=1, device_id={"node": sibling}, device_id_type=MESH)
    pl.semaphore_wait(barrier, chips)

    rows = pl.ds(pl.multiple_of(core * half, half), half)
    sources = (gu_ref.at[0], dw_ref)
    places = (weights.at[pl.ds(0, 2), rows], weights.at[pl.ds(2, 1), rows])
    local_copies = []
    sibling_copies = []
    for i in range(2):
        local_copies.append(pltpu.make_async_copy(sources[i], places[i], w_local.at[i]))
        sibling_copies.append(
            pltpu.make_async_remote_copy(
                src_ref=sources[i], dst_ref=places[i], send_sem=w_send.at[i], recv_sem=w_recv.at[i],
                device_id={"node": sibling}, device_id_type=MESH,
            )
        )
    col_iota = lax.broadcasted_iota(jnp.int32, (chips, tok_rows), 0)
    ohs = [(routes_t_ref[k : k + 1, :] == col_iota).astype(jnp.float32) for k in range(2)]
    earlier = (
        lax.broadcasted_iota(jnp.int32, (tok_rows, tok_rows), 0)
        < lax.broadcasted_iota(jnp.int32, (tok_rows, tok_rows), 1)
    ).astype(jnp.float32)
    before = jnp.dot(
        (ohs[0] + ohs[1]).astype(jnp.bfloat16), earlier.astype(jnp.bfloat16), preferred_element_type=jnp.float32
    )
    slots = [jnp.sum(ohs[k] * before, axis=0, keepdims=True).astype(jnp.int32) for k in range(2)]
    slot_iota = lax.broadcasted_iota(jnp.int32, (capacity, tok_rows), 0)

    def pack(expert):
        picks = [
            ((slots[k] == slot_iota) & (routes_t_ref[k : k + 1, :] == expert)).astype(jnp.float32) for k in range(2)
        ]
        pick = (picks[0] + picks[1]).astype(jnp.bfloat16)
        row_gate = jnp.sum(picks[0] * gates_t_ref[0:1, :] + picks[1] * gates_t_ref[1:2, :], axis=1, keepdims=True)
        packed[expert, 0] = jnp.dot(pick, tok_ref[...], preferred_element_type=jnp.float32).astype(jnp.bfloat16)
        cot_rows = jnp.dot(pick, cot_ref[...], preferred_element_type=jnp.float32)
        packed[expert, 1] = (cot_rows * row_gate).astype(jnp.bfloat16)

    def send_in(step):
        return pltpu.make_async_remote_copy(
            src_ref=packed.at[flip(chip, step)], dst_ref=arrived.at[step],
            send_sem=in_send.at[step], recv_sem=in_recv.at[step], device_id=device(step), device_id_type=MESH,
        )

    def send_back(step):
        return pltpu.make_async_remote_copy(
            src_ref=results.at[step], dst_ref=returned.at[chip],
            send_sem=back_send.at[step], recv_sem=back_recv.at[step], device_id=device(step), device_id_type=MESH,
        )

    for i, step in enumerate(SEND_ORDER):
        pack(flip(chip, step))
        send_in(step).start()
        if i == 0:
            for copy in local_copies + sibling_copies:
                copy.start()
    pack(chip)
    own = pltpu.make_async_copy(packed.at[chip], arrived.at[0], self_sem.at[0])
    own.start()

    def hidden_tile(first, start, width):
        rows_in = 2 * capacity
        inputs = arrived[first : first + 2, 0].reshape(rows_in, features)
        scaled = arrived[first : first + 2, 1].reshape(rows_in, features)
        gate_w = weights[0, pl.ds(start, width), :]
        up_w = weights[1, pl.ds(start, width), :]
        down_w = weights[2, pl.ds(start, width), :]
        across = (((1,), (1,)), ((), ()))
        gate = lax.dot_general(inputs, gate_w, across, preferred_element_type=jnp.float32)
        up = lax.dot_general(inputs, up_w, across, preferred_element_type=jnp.float32)
        d_hidden = lax.dot_general(scaled, down_w, across, preferred_element_type=jnp.float32)
        sig = jax.nn.sigmoid(gate)
        act = gate * sig
        hidden = (act * up).astype(jnp.bfloat16)
        d_gate = (d_hidden * up * sig * (1.0 + gate * (1.0 - sig))).astype(jnp.bfloat16)
        d_up = (d_hidden * act).astype(jnp.bfloat16)
        out = jnp.dot(hidden, down_w, preferred_element_type=jnp.float32)
        grad = jnp.dot(d_gate, gate_w, preferred_element_type=jnp.float32)
        grad += jnp.dot(d_up, up_w, preferred_element_type=jnp.float32)
        return out, grad

    full = units // TILE
    rest = units - full * TILE
    for n, first in enumerate(BATCHES):
        if n == 0:
            own.wait()
            for copy in local_copies:
                copy.wait()
            for copy in sibling_copies:
                copy.wait_recv()
        for step in (first, first + 1):
            if step:
                send_in(step).wait_recv()
        acc_out[...], acc_grad[...] = hidden_tile(first, 0, TILE)

        def body(t, carry):
            out, grad = hidden_tile(first, pl.multiple_of(t * TILE, TILE), TILE)
            acc_out[...] += out
            acc_grad[...] += grad
            return carry

        lax.fori_loop(1, full, body, 0)
        if rest:
            out, grad = hidden_tile(first, full * TILE, rest)
            acc_out[...] += out
            acc_grad[...] += grad
        shape = (2, capacity, features)
        results[first : first + 2, 0] = acc_out[...].astype(jnp.bfloat16).reshape(shape)
        results[first : first + 2, 1] = acc_grad[...].astype(jnp.bfloat16).reshape(shape)
        for step in (first, first + 1):
            if step:
                send_back(step).start()
    own_back = pltpu.make_async_copy(results.at[0], returned.at[chip], self_sem.at[1])
    own_back.start()

    exp_iota = lax.broadcasted_iota(jnp.int32, (tok_rows, chips), 1)
    oh_cols = [(routes_ref[:, k : k + 1] == exp_iota).astype(jnp.float32) for k in range(2)]
    later = (
        lax.broadcasted_iota(jnp.int32, (tok_rows, tok_rows), 1)
        < lax.broadcasted_iota(jnp.int32, (tok_rows, tok_rows), 0)
    ).astype(jnp.float32)
    before_cols = jnp.dot(
        later.astype(jnp.bfloat16), (oh_cols[0] + oh_cols[1]).astype(jnp.bfloat16), preferred_element_type=jnp.float32
    )
    all_rows = chips * capacity
    place_iota = lax.broadcasted_iota(jnp.int32, (tok_rows, all_rows), 1)
    selects = []
    for k in range(2):
        slot = jnp.sum(oh_cols[k] * before_cols, axis=1, keepdims=True).astype(jnp.int32)
        place = routes_ref[:, k : k + 1] * capacity + slot
        selects.append((place == place_iota).astype(jnp.float32).astype(jnp.bfloat16))
    both = selects[0] + selects[1]

    own_back.wait()
    for step in range(1, chips):
        send_back(step).wait_recv()
    gate_cols = [gates_ref[:, k : k + 1] for k in range(2)]
    sums = [jnp.zeros((tok_rows, 1), jnp.float32) for _ in range(2)]
    width = features // 4
    for j in range(4):
        cols = slice(j * width, (j + 1) * width)
        outs = returned[:, 0, :, cols].reshape(all_rows, width)
        grads = returned[:, 1, :, cols].reshape(all_rows, width)
        cot = cot_ref[:, cols].astype(jnp.float32)
        pairs = [jnp.dot(selects[k], outs, preferred_element_type=jnp.float32) for k in range(2)]
        out_ref[:, cols] = (gate_cols[0] * pairs[0] + gate_cols[1] * pairs[1]).astype(jnp.bfloat16)
        for k in range(2):
            sums[k] += jnp.sum(cot * pairs[k], axis=1, keepdims=True)
        tgrad_ref[:, cols] = jnp.dot(both, grads, preferred_element_type=jnp.float32).astype(jnp.bfloat16)
    ggrad_ref[...] = jnp.concatenate(sums, axis=1)

    for copy in sibling_copies:
        copy.wait_send()
    for step in range(1, chips):
        send_in(step).wait_send()
        send_back(step).wait_send()


def exchange_once(tokens, routes, gate_values, cotangent, gate_up, down_weight):
    tok_rows, chosen = routes.shape
    features = tokens.shape[1]
    chips = lax.axis_size("node") // 2
    capacity = 3 * tok_rows * chosen // (2 * chips)
    half = down_weight.shape[1]
    vmem = pl.BlockSpec(memory_space=pltpu.VMEM)
    hbm = pl.BlockSpec(memory_space=pl.ANY)
    rows = pltpu.VMEM((chips, 2, capacity, features), jnp.bfloat16)
    total = pltpu.VMEM((2 * capacity, features), jnp.float32)
    dma = pltpu.SemaphoreType.DMA
    flops = 2 * chips * capacity * features * half * 12
    return pl.pallas_call(
        functools.partial(kernel, chips, capacity),
        out_shape=(
            jax.ShapeDtypeStruct(tokens.shape, tokens.dtype),
            jax.ShapeDtypeStruct(tokens.shape, tokens.dtype),
            jax.ShapeDtypeStruct(gate_values.shape, jnp.float32),
        ),
        in_specs=[vmem] * 6 + [hbm] * 2,
        out_specs=(vmem, vmem, vmem),
        scratch_shapes=[
            pltpu.VMEM((3, 2 * half, features), jnp.bfloat16),
            rows, rows, rows, rows, total, total,
            dma((2,)), dma((2,)), dma((2,)),
            dma((chips,)), dma((chips,)), dma((chips,)), dma((chips,)), dma((2,)),
        ],
        compiler_params=pltpu.CompilerParams(
            collective_id=0, has_side_effects=True, vmem_limit_bytes=56 * 1024 * 1024
        ),
        cost_estimate=pl.CostEstimate(flops=flops, bytes_accessed=12 * half * features, transcendentals=0),
    )(tokens, cotangent, routes, routes.T, gate_values, gate_values.T, gate_up, down_weight)


def exchange_whole(tokens, routes, gate_values, cotangent, gate_up, down_weight):
    tok_rows, chosen = routes.shape
    features = tokens.shape[1]
    experts = lax.axis_size("node") // 2
    capacity = 3 * tok_rows * chosen // (2 * experts)
    pair_count = tok_rows * chosen
    expert = routes.reshape(pair_count)
    onehot = (expert[:, None] == jnp.arange(experts, dtype=jnp.int32)[None, :]).astype(jnp.int32)
    before = jnp.cumsum(onehot, axis=0) - onehot
    slot_index = jnp.sum(before * onehot, axis=1)
    column = expert * capacity + slot_index
    select = (column[:, None] == jnp.arange(experts * capacity, dtype=jnp.int32)[None, :]).astype(
        jnp.bfloat16
    )

    def pack_rows(pair_rows):
        packed = lax.dot_general(
            select, pair_rows, (((0,), (0,)), ((), ())), preferred_element_type=jnp.float32
        )
        return packed.astype(jnp.bfloat16).reshape(experts, capacity, features)

    def unpack_rows(buffer_rows):
        return jnp.dot(
            select,
            buffer_rows.reshape(experts * capacity, features),
            preferred_element_type=jnp.float32,
        )

    def deliver(stacked):
        doubled = jnp.repeat(stacked, 2, axis=1)
        return lax.all_to_all(doubled, "node", split_axis=1, concat_axis=1, tiled=True)

    def collect(partials):
        returned = lax.all_to_all(partials, "node", split_axis=0, concat_axis=0, tiled=True)
        summed = jnp.sum(
            returned.reshape(experts, 2, capacity, features).astype(jnp.float32), axis=1
        )
        return summed.astype(jnp.bfloat16)

    token_pairs = jnp.repeat(tokens, chosen, axis=0)
    gate_flat = gate_values.reshape(pair_count)
    cot_pairs = jnp.repeat(cotangent, chosen, axis=0).astype(jnp.float32)
    scaled_pairs = (gate_flat[:, None] * cot_pairs).astype(jnp.bfloat16)
    inputs = deliver(pack_rows(token_pairs)[None])[0]
    weights = gate_up.reshape(-1, features)
    half_units = weights.shape[0] // 2
    down_rows = down_weight.reshape(half_units, features)
    buffer_rows = inputs.reshape(-1, features)
    projected = lax.dot_general(
        buffer_rows, weights, (((1,), (1,)), ((), ())), preferred_element_type=jnp.float32
    )
    gate_part = projected[:, :half_units]
    up_part = projected[:, half_units:]
    sigmoid_gate = jax.nn.sigmoid(gate_part)
    activated = gate_part * sigmoid_gate
    hidden = (activated * up_part).astype(jnp.bfloat16)
    partial_out = jnp.dot(hidden, down_rows, preferred_element_type=jnp.float32).astype(
        jnp.bfloat16
    )
    out_pairs = unpack_rows(collect(partial_out.reshape(inputs.shape)))
    layer_out = jnp.sum(
        (gate_flat[:, None] * out_pairs).reshape(tok_rows, chosen, features), axis=1
    ).astype(jnp.bfloat16)
    gate_grad = jnp.sum(cot_pairs * out_pairs, axis=1).reshape(tok_rows, chosen)
    grads_in = deliver(pack_rows(scaled_pairs)[None])[0]
    signal = grads_in.reshape(-1, features)
    d_hidden = lax.dot_general(
        signal, down_rows, (((1,), (1,)), ((), ())), preferred_element_type=jnp.float32
    )
    d_gate = d_hidden * up_part * sigmoid_gate * (1.0 + gate_part * (1.0 - sigmoid_gate))
    d_up = d_hidden * activated
    d_both = jnp.concatenate([d_gate, d_up], axis=1).astype(jnp.bfloat16)
    d_partial = jnp.dot(d_both, weights, preferred_element_type=jnp.float32).astype(jnp.bfloat16)
    grad_pairs = unpack_rows(collect(d_partial.reshape(inputs.shape)))
    token_grad = jnp.sum(grad_pairs.reshape(tok_rows, chosen, features), axis=1).astype(
        jnp.bfloat16
    )
    return (layer_out, token_grad, gate_grad)


def local(*args):
    routes = args[1]
    chips = lax.axis_size("node") // 2
    slots = 3 * routes.shape[0] * routes.shape[1]
    if chips == 8 and slots % (2 * chips) == 0 and slots // (2 * chips) % 16 == 0:
        return exchange_once(*args)
    return exchange_whole(*args)


def solution(mesh):
    placed = (
        P(("groups", "node"), None),
        P(("groups", "node"), None),
        P(("groups", "node"), None),
        P(("groups", "node"), None),
        P("node", None, None, None),
        P("node", None, None),
    )
    return jax.shard_map(
        local,
        mesh=mesh,
        in_specs=placed,
        out_specs=(
            P(("groups", "node"), None),
            P(("groups", "node"), None),
            P(("groups", "node"), None),
        ),
        check_vma=False,
    )
```

```python
import functools

import jax
import jax.numpy as jnp
from jax import lax
from jax.experimental import pallas as pl
from jax.experimental.pallas import tpu as pltpu
from jax.sharding import PartitionSpec as P

MESH = pl.DeviceIdType.MESH
NEAR = 4
PARTNER = 6
TILE = 256
TOK, COT, META, OUT, GRAD, GATE = range(6)


def flip(index, step):
    bit = 1
    while bit <= step:
        if step & bit:
            index = index + (1 - 2 * ((index // bit) % 2)) * bit
        bit *= 2
    return index


def kernel(
    capacity, chips, tok_ref, cot_ref, meta_ref, gu_ref, dw_ref,
    out_ref, tgrad_ref, ggrad_ref,
    weights, raw, meta_in, packed, arrived, results, returned,
    gates, ups, acc, own_out, own_grad, far_out, far_in, gate_out, gate_in,
    w_local, w_send, w_recv, in_send, in_recv, back_send, back_recv, far_send, far_recv, self_sem,
):
    tok_rows, features = tok_ref.shape
    half = dw_ref.shape[1]
    units = 2 * half
    rows = NEAR * capacity
    node = lax.axis_index("node")
    chip = node // 2
    core = node % 2
    sibling = {"node": chip * 2 + 1 - core}

    def device(step):
        return {"node": flip(chip, step) * 2 + core}

    barrier = pltpu.get_barrier_semaphore()
    for other in (device(1), device(2), device(3), device(PARTNER), sibling):
        pl.semaphore_signal(barrier, inc=1, device_id=other, device_id_type=MESH)
    pl.semaphore_wait(barrier, NEAR + 1)

    def far(which):
        source, target = (
            (tok_ref, raw.at[0]), (cot_ref, raw.at[1]), (meta_ref, meta_in),
            (far_out.at[0], far_in.at[0]), (far_out.at[1], far_in.at[1]), (gate_out, gate_in),
        )[which]
        return pltpu.make_async_remote_copy(
            src_ref=source, dst_ref=target, send_sem=far_send.at[which], recv_sem=far_recv.at[which],
            device_id=device(PARTNER), device_id_type=MESH,
        )

    def send_in(load, kind, step):
        sem = (load * 2 + kind) * NEAR + step
        return pltpu.make_async_remote_copy(
            src_ref=packed.at[load, kind, step], dst_ref=arrived.at[load, kind, step],
            send_sem=in_send.at[sem], recv_sem=in_recv.at[sem], device_id=device(step), device_id_type=MESH,
        )

    def send_back(load, kind, step):
        sem = (load * 2 + kind) * NEAR + step
        return pltpu.make_async_remote_copy(
            src_ref=results.at[load, kind, step], dst_ref=returned.at[load, kind, step],
            send_sem=back_send.at[sem], recv_sem=back_recv.at[sem], device_id=device(step), device_id_type=MESH,
        )

    far(META).start()
    far(TOK).start()

    def slots_of(meta):
        experts = lax.broadcasted_iota(jnp.int32, (chips, tok_rows), 0).astype(jnp.float32)
        ohs = [(meta[k : k + 1, :] == experts).astype(jnp.float32) for k in range(2)]
        earlier = (
            lax.broadcasted_iota(jnp.int32, (tok_rows, tok_rows), 0)
            < lax.broadcasted_iota(jnp.int32, (tok_rows, tok_rows), 1)
        ).astype(jnp.float32)
        before = jnp.dot(
            (ohs[0] + ohs[1]).astype(jnp.bfloat16), earlier.astype(jnp.bfloat16), preferred_element_type=jnp.float32
        )
        return [jnp.sum(oh * before, axis=0, keepdims=True) for oh in ohs]

    slot_iota = lax.broadcasted_iota(jnp.int32, (capacity, tok_rows), 0).astype(jnp.float32)

    def pack(load, kind, meta, slots, source):
        for step in (1, 2, 3, 0):
            expert = flip(chip, step).astype(jnp.float32)
            picks = [
                ((slots[k] == slot_iota) & (meta[k : k + 1, :] == expert)).astype(jnp.float32) for k in range(2)
            ]
            pick = (picks[0] + picks[1]).astype(jnp.bfloat16)
            chosen = jnp.dot(pick, source, preferred_element_type=jnp.float32)
            if kind == 1:
                chosen = chosen * jnp.sum(picks[0] * meta[2:3, :] + picks[1] * meta[3:4, :], axis=1, keepdims=True)
            if step:
                packed[load, kind, step] = chosen.astype(jnp.bfloat16)
                send_in(load, kind, step).start()
            else:
                arrived[load, kind, 0] = chosen.astype(jnp.bfloat16)

    own_meta = meta_ref[...]
    own_slots = slots_of(own_meta)
    pack(0, 0, own_meta, own_slots, tok_ref[...])
    place = pl.ds(pl.multiple_of(core * half, half), half)
    sources = (gu_ref.at[0], dw_ref)
    places = (weights.at[pl.ds(0, 2), place], weights.at[pl.ds(2, 1), place])
    local_copies = []
    sibling_copies = []
    for i in range(2):
        local_copies.append(pltpu.make_async_copy(sources[i], places[i], w_local.at[i]))
        sibling_copies.append(
            pltpu.make_async_remote_copy(
                src_ref=sources[i], dst_ref=places[i], send_sem=w_send.at[i], recv_sem=w_recv.at[i],
                device_id=sibling, device_id_type=MESH,
            )
        )
    for copy in local_copies + sibling_copies:
        copy.start()

    across = (((1,), (1,)), ((), ()))

    def forward(load, start, width):
        inputs = arrived[load, 0].reshape(rows, features)
        spot = pl.ds(start, width)
        gate = lax.dot_general(inputs, weights[0, spot, :], across, preferred_element_type=jnp.float32)
        up = lax.dot_general(inputs, weights[1, spot, :], across, preferred_element_type=jnp.float32)
        gates[load, :, spot] = gate
        ups[load, :, spot] = up
        hidden = (gate * jax.nn.sigmoid(gate) * up).astype(jnp.bfloat16)
        return jnp.dot(hidden, weights[2, spot, :], preferred_element_type=jnp.float32)

    def backward(load, start, width):
        scaled = arrived[load, 1].reshape(rows, features)
        spot = pl.ds(start, width)
        d_hidden = lax.dot_general(scaled, weights[2, spot, :], across, preferred_element_type=jnp.float32)
        gate = gates[load, :, spot]
        up = ups[load, :, spot]
        sig = jax.nn.sigmoid(gate)
        d_gate = (d_hidden * up * sig * (1.0 + gate * (1.0 - sig))).astype(jnp.bfloat16)
        d_up = (d_hidden * gate * sig).astype(jnp.bfloat16)
        grad = jnp.dot(d_gate, weights[0, spot, :], preferred_element_type=jnp.float32)
        return grad + jnp.dot(d_up, weights[1, spot, :], preferred_element_type=jnp.float32)

    full = units // TILE
    rest = units - full * TILE

    def run(load, kind):
        stage = (forward, backward)[kind]
        for step in range(1, NEAR):
            send_in(load, kind, step).wait_recv()
        acc[...] = stage(load, 0, TILE)

        def body(t, carry):
            acc[...] += stage(load, pl.multiple_of(t * TILE, TILE), TILE)
            return carry

        lax.fori_loop(1, full, body, 0)
        if rest:
            acc[...] += stage(load, full * TILE, rest)
        done = acc[...].astype(jnp.bfloat16).reshape(NEAR, capacity, features)
        results[load, kind] = done
        for step in range(1, NEAR):
            send_back(load, kind, step).start()
        returned[load, kind, 0] = done[0]

    far(TOK).wait_send()
    far(COT).start()
    far(META).wait_recv()
    far(TOK).wait_recv()
    far_meta = meta_in[...]
    far_slots = slots_of(far_meta)
    pack(1, 0, far_meta, far_slots, raw[0])
    pack(0, 1, own_meta, own_slots, cot_ref[...])
    for copy in local_copies:
        copy.wait()
    for copy in sibling_copies:
        copy.wait_recv()
    run(0, 0)
    run(1, 0)
    far(COT).wait_recv()
    pack(1, 1, far_meta, far_slots, raw[1])
    run(0, 1)

    token_iota = lax.broadcasted_iota(jnp.int32, (tok_rows, tok_rows), 0)
    eye = token_iota == lax.broadcasted_iota(jnp.int32, (tok_rows, tok_rows), 1)

    def column(row):
        return jnp.sum(jnp.where(eye, row, 0.0), axis=1, keepdims=True)

    row_iota = lax.broadcasted_iota(jnp.int32, (tok_rows, rows), 1)
    row_expert = jnp.zeros((tok_rows, rows), jnp.float32)
    for step in range(NEAR):
        row_expert = jnp.where(row_iota // capacity == step, flip(chip, step).astype(jnp.float32), row_expert)
    row_slot = (row_iota % capacity).astype(jnp.float32)

    def selects_of(meta, slots):
        return [
            ((column(meta[k : k + 1, :]) == row_expert) & (column(slots[k]) == row_slot))
            .astype(jnp.float32).astype(jnp.bfloat16)
            for k in range(2)
        ]

    width = features // 4
    lane_iota = lax.broadcasted_iota(jnp.int32, (tok_rows, 128), 1)

    def combine_out(load, selects, meta, cotangent, target):
        for step in range(1, NEAR):
            send_back(load, 0, step).wait_recv()
        gate_cols = [column(meta[2 + k : 3 + k, :]) for k in range(2)]
        sums = [jnp.zeros((tok_rows, 1), jnp.float32) for _ in range(2)]
        for j in range(4):
            cols = slice(j * width, (j + 1) * width)
            outs = returned[load, 0, :, :, cols].reshape(rows, width)
            cot = cotangent[:, cols].astype(jnp.float32)
            pairs = [jnp.dot(selects[k], outs, preferred_element_type=jnp.float32) for k in range(2)]
            target[:, cols] = (gate_cols[0] * pairs[0] + gate_cols[1] * pairs[1]).astype(target.dtype)
            for k in range(2):
                sums[k] += jnp.sum(cot * pairs[k], axis=1, keepdims=True)
        return jnp.where(lane_iota == 0, sums[0], jnp.where(lane_iota == 1, sums[1], 0.0))

    def combine_grad(load, selects, target):
        for step in range(1, NEAR):
            send_back(load, 1, step).wait_recv()
        both = selects[0] + selects[1]
        for j in range(4):
            cols = slice(j * width, (j + 1) * width)
            grads = returned[load, 1, :, :, cols].reshape(rows, width)
            target[:, cols] = jnp.dot(both, grads, preferred_element_type=jnp.float32).astype(target.dtype)

    far_selects = selects_of(far_meta, far_slots)
    gate_out[...] = combine_out(1, far_selects, far_meta, raw.at[1], far_out.at[0])
    far(OUT).start()
    far(GATE).start()
    run(1, 1)
    own_selects = selects_of(own_meta, own_slots)
    own_gate = combine_out(0, own_selects, own_meta, cot_ref, own_out)
    combine_grad(1, far_selects, far_out.at[1])
    far(GRAD).start()
    combine_grad(0, own_selects, own_grad)
    far(GATE).wait_recv()
    ggrad_ref[...] = (own_gate + gate_in[...])[:, 0:2]
    far(OUT).wait_recv()
    out_ref[...] = (own_out[...] + far_in[0].astype(jnp.float32)).astype(jnp.bfloat16)
    far(GRAD).wait_recv()
    tgrad_ref[...] = (own_grad[...] + far_in[1].astype(jnp.float32)).astype(jnp.bfloat16)

    for copy in sibling_copies:
        copy.wait_send()
    for which in (COT, META, OUT, GRAD, GATE):
        far(which).wait_send()
    for load in range(2):
        for kind in range(2):
            for step in range(1, NEAR):
                send_in(load, kind, step).wait_send()
                send_back(load, kind, step).wait_send()


def exchange_once(tokens, routes, gate_values, cotangent, gate_up, down_weight):
    tok_rows, chosen = routes.shape
    features = tokens.shape[1]
    chips = lax.axis_size("node") // 2
    capacity = 3 * tok_rows * chosen // (2 * chips)
    half = down_weight.shape[1]
    rows = NEAR * capacity
    meta = jnp.concatenate(
        [routes.T.astype(jnp.float32), gate_values.T, jnp.zeros((4, tok_rows), jnp.float32)], axis=0
    )
    vmem = pl.BlockSpec(memory_space=pltpu.VMEM)
    hbm = pl.BlockSpec(memory_space=pl.ANY)
    buffers = pltpu.VMEM((2, 2, NEAR, capacity, features), jnp.bfloat16)
    pair = pltpu.VMEM((2, tok_rows, features), jnp.bfloat16)
    total = pltpu.VMEM((tok_rows, features), jnp.float32)
    hidden = pltpu.VMEM((2, rows, 2 * half), jnp.float32)
    lanes = pltpu.VMEM((tok_rows, 128), jnp.float32)
    dma = pltpu.SemaphoreType.DMA
    flops = 2 * chips * capacity * features * half * 12
    return pl.pallas_call(
        functools.partial(kernel, capacity, chips),
        out_shape=(
            jax.ShapeDtypeStruct(tokens.shape, tokens.dtype),
            jax.ShapeDtypeStruct(tokens.shape, tokens.dtype),
            jax.ShapeDtypeStruct(gate_values.shape, jnp.float32),
        ),
        in_specs=[vmem] * 3 + [hbm] * 2,
        out_specs=(vmem, vmem, vmem),
        scratch_shapes=[
            pltpu.VMEM((3, 2 * half, features), jnp.bfloat16),
            pair, pltpu.VMEM(meta.shape, jnp.float32), buffers, buffers, buffers, buffers,
            hidden, hidden, pltpu.VMEM((rows, features), jnp.float32), total, total, pair, pair, lanes, lanes,
            dma((2,)), dma((2,)), dma((2,)),
            dma((4 * NEAR,)), dma((4 * NEAR,)), dma((4 * NEAR,)), dma((4 * NEAR,)), dma((6,)), dma((6,)), dma((2,)),
        ],
        compiler_params=pltpu.CompilerParams(
            collective_id=0, has_side_effects=True, vmem_limit_bytes=58 * 1024 * 1024
        ),
        cost_estimate=pl.CostEstimate(flops=flops, bytes_accessed=12 * half * features, transcendentals=0),
    )(tokens, cotangent, meta, gate_up, down_weight)


def exchange_whole(tokens, routes, gate_values, cotangent, gate_up, down_weight):
    tok_rows, chosen = routes.shape
    features = tokens.shape[1]
    experts = lax.axis_size("node") // 2
    capacity = 3 * tok_rows * chosen // (2 * experts)
    pair_count = tok_rows * chosen
    expert = routes.reshape(pair_count)
    onehot = (expert[:, None] == jnp.arange(experts, dtype=jnp.int32)[None, :]).astype(jnp.int32)
    before = jnp.cumsum(onehot, axis=0) - onehot
    slot_index = jnp.sum(before * onehot, axis=1)
    column = expert * capacity + slot_index
    select = (column[:, None] == jnp.arange(experts * capacity, dtype=jnp.int32)[None, :]).astype(
        jnp.bfloat16
    )

    def pack_rows(pair_rows):
        packed = lax.dot_general(
            select, pair_rows, (((0,), (0,)), ((), ())), preferred_element_type=jnp.float32
        )
        return packed.astype(jnp.bfloat16).reshape(experts, capacity, features)

    def unpack_rows(buffer_rows):
        return jnp.dot(
            select,
            buffer_rows.reshape(experts * capacity, features),
            preferred_element_type=jnp.float32,
        )

    def deliver(stacked):
        doubled = jnp.repeat(stacked, 2, axis=1)
        return lax.all_to_all(doubled, "node", split_axis=1, concat_axis=1, tiled=True)

    def collect(partials):
        returned = lax.all_to_all(partials, "node", split_axis=0, concat_axis=0, tiled=True)
        summed = jnp.sum(
            returned.reshape(experts, 2, capacity, features).astype(jnp.float32), axis=1
        )
        return summed.astype(jnp.bfloat16)

    token_pairs = jnp.repeat(tokens, chosen, axis=0)
    gate_flat = gate_values.reshape(pair_count)
    cot_pairs = jnp.repeat(cotangent, chosen, axis=0).astype(jnp.float32)
    scaled_pairs = (gate_flat[:, None] * cot_pairs).astype(jnp.bfloat16)
    inputs = deliver(pack_rows(token_pairs)[None])[0]
    weights = gate_up.reshape(-1, features)
    half_units = weights.shape[0] // 2
    down_rows = down_weight.reshape(half_units, features)
    buffer_rows = inputs.reshape(-1, features)
    projected = lax.dot_general(
        buffer_rows, weights, (((1,), (1,)), ((), ())), preferred_element_type=jnp.float32
    )
    gate_part = projected[:, :half_units]
    up_part = projected[:, half_units:]
    sigmoid_gate = jax.nn.sigmoid(gate_part)
    activated = gate_part * sigmoid_gate
    hidden = (activated * up_part).astype(jnp.bfloat16)
    partial_out = jnp.dot(hidden, down_rows, preferred_element_type=jnp.float32).astype(
        jnp.bfloat16
    )
    out_pairs = unpack_rows(collect(partial_out.reshape(inputs.shape)))
    layer_out = jnp.sum(
        (gate_flat[:, None] * out_pairs).reshape(tok_rows, chosen, features), axis=1
    ).astype(jnp.bfloat16)
    gate_grad = jnp.sum(cot_pairs * out_pairs, axis=1).reshape(tok_rows, chosen)
    grads_in = deliver(pack_rows(scaled_pairs)[None])[0]
    signal = grads_in.reshape(-1, features)
    d_hidden = lax.dot_general(
        signal, down_rows, (((1,), (1,)), ((), ())), preferred_element_type=jnp.float32
    )
    d_gate = d_hidden * up_part * sigmoid_gate * (1.0 + gate_part * (1.0 - sigmoid_gate))
    d_up = d_hidden * activated
    d_both = jnp.concatenate([d_gate, d_up], axis=1).astype(jnp.bfloat16)
    d_partial = jnp.dot(d_both, weights, preferred_element_type=jnp.float32).astype(jnp.bfloat16)
    grad_pairs = unpack_rows(collect(d_partial.reshape(inputs.shape)))
    token_grad = jnp.sum(grad_pairs.reshape(tok_rows, chosen, features), axis=1).astype(
        jnp.bfloat16
    )
    return (layer_out, token_grad, gate_grad)


def local(*args):
    routes = args[1]
    chips = lax.axis_size("node") // 2
    slots = 3 * routes.shape[0] * routes.shape[1]
    if chips == 2 * NEAR and routes.shape[0] == 128 and slots % (2 * chips) == 0 and slots // (2 * chips) % 16 == 0:
        return exchange_once(*args)
    return exchange_whole(*args)


def solution(mesh):
    placed = (
        P(("groups", "node"), None),
        P(("groups", "node"), None),
        P(("groups", "node"), None),
        P(("groups", "node"), None),
        P("node", None, None, None),
        P("node", None, None),
    )
    return jax.shard_map(
        local,
        mesh=mesh,
        in_specs=placed,
        out_specs=(
            P(("groups", "node"), None),
            P(("groups", "node"), None),
            P(("groups", "node"), None),
        ),
        check_vma=False,
    )
```
